32 devices in a mesh: wa: 8 (over z, x), af: 4 (over y, core).
Axes of the slice: x: 2, y: 2, z: 4, core: 2. Of those that a mesh axis runs over, the one named last changes fastest.
Arguments:
- spectra: bfloat16 [80, 80, 128], P('wa', None, 'af'), may hold values from -6 to 6
- legendre: bfloat16 [80, 80, 8], P('wa', 'af'), may hold values from -0.625 to 0.625
- wave_of_slot: int32 [80], replicated, may hold values from 0 to 79, each once
- row_points: int32 [8], P('wa'), may hold values from 2560 to 5120, as said below
- row_weight: float32 [8], P('wa'), may hold values from 0.1 to 1.5, as said below
- soil_water: float32 [8, 4, 5120], P('wa', None, 'af'), may hold values from 0.02 to 0.48
- land_mask: int32 [8, 5120], P('wa', 'af'), may hold values 0 or 1
- soil_type: int32 [8, 5120], P('wa', 'af'), may hold values from 0 to 6
- plant_type: int32 [8, 5120], P('wa', 'af'), may hold values from 0 to 19
- soil_params: float32 [2, 7], replicated, may hold values from 0 to 1
- root_profile: float32 [20, 4], replicated, may hold values from 0.1 to 10
Outputs:
- grid_fields: bfloat16 [8, 64, 5120], P('wa', None, 'af')
- uptake: float32 [8, 4, 5120], P('wa', None, 'af')
- spectral_fluxes: float32 [80, 8, 80], P('wa', None, 'af')
The draws below stay inside these ranges and needn't reach their ends.
Inputs may be any that keep to these rules, and one draw needn't show every extreme that they name: `wave_of_slot`: each slot number from 0 to 79 is named once. `row_points`: every count is a multiple of 4; some row has exactly 5120 points and some row exactly 2560. `row_weight`: positive weights.
All inputs are finite; a program needn't handle non-finite values. No bound on the sum of `land_mask` on one device may be relied on, other than what follows from the above.
Results may differ from the reference program's by a relative error of at most 0.009.
Values may be sent and summed in bfloat16 or wider, within the bound.
A program may use at most 64 MiB of HBM per device.

```python
import math
import jax
import jax.numpy as jnp
from jax import lax

LEVELS = 8
NLON = 5120
FLUXES = 4
SOIL_LAYERS = 4
SOIL_TYPES = 7
PLANT_TYPES = 20
M = 80
NJ = 80
NLAT = 8
FL = 64
COLS = 128
GROUP = 16


def draw_row_points(key, part):
    key_steps, key_top, key_low = jax.random.split(key, 3)
    steps_down = jax.random.randint(key_steps, (NLAT,), 0, NLON // 8 + 1)
    counts = NLON - 4 * steps_down
    rows = jnp.arange(NLAT)
    top_row = jax.random.randint(key_top, (), 0, NLAT)
    low_row = (top_row + 1 + jax.random.randint(key_low, (), 0, NLAT - 1)) % NLAT
    counts = jnp.where(rows == top_row, NLON, counts)
    counts = jnp.where(rows == low_row, NLON // 2, counts)
    return counts.astype(jnp.int32)


def draw_row_weight(key, part):
    rows = jnp.arange(NLAT).astype(jnp.float32)
    base = 0.25 + 0.75 * (rows + 0.5) / NLAT
    jitter = jnp.exp(jax.random.uniform(key, (NLAT,), jnp.float32, -0.3, 0.3))
    return (base * jitter).astype(jnp.float32)


def touch_ends(entries, key, least, top_value):
    place = [jax.random.randint(jax.random.fold_in(key, axis), (), 0, length) for axis, length in enumerate(entries.shape)]
    longest = entries.shape.index(max(entries.shape))
    next_to = place[:longest] + [(place[longest] + 1) % entries.shape[longest]] + place[longest + 1:]
    return entries.at[tuple(place)].set(least).at[tuple(next_to)].set(top_value)


def shard_levels(stream_key, shape, pieces, low, high):
    gain = 1.0
    for dim, blocks in pieces:
        draws = jax.random.uniform(jax.random.fold_in(jax.random.fold_in(stream_key, 6), dim), (blocks,), jnp.float32, low / len(pieces), high / len(pieces))
        gain = gain * jnp.repeat(jnp.exp(draws), shape[dim] // blocks).reshape((-1,) + (1,) * (len(shape) - 1 - dim))
    return gain


def noise(key, shape, width, reach, cuts=(), kind=jnp.bfloat16):
    level = shard_levels(key, shape, cuts, -0.22, 0.18) if cuts else 1.0
    values = jax.random.normal(key, shape, jnp.float32) * width * level
    return jnp.minimum(jnp.maximum(values, -reach), reach).astype(kind)


def setup_inputs(seed: int = 0) -> dict:
    streams_of = jax.random.split(jax.random.key(seed), 12)
    spectra = noise(streams_of[0], (M, NJ, COLS), 1.0, 6.0, ((0, 8), (2, 4)))
    legendre = noise(streams_of[1], (M, NJ, NLAT), NJ ** -0.5, 0.625, ((0, 8), (1, 4)))
    wave_of_slot = jax.random.permutation(streams_of[2], M).astype(jnp.int32)
    row_points = draw_row_points(jax.random.fold_in(streams_of[11], 71), 0)
    row_weight = draw_row_weight(jax.random.fold_in(streams_of[11], 71), 0)
    soil_water = jnp.clip(0.02 + 0.45999999 * jax.random.uniform(streams_of[5], (NLAT, SOIL_LAYERS, NLON), jnp.float32) ** shard_levels(streams_of[5], (NLAT, SOIL_LAYERS, NLON), ((0, 8), (2, 4)), -0.2, 0.2), 0.02, 0.48)
    land_mask = touch_ends((jax.random.randint(streams_of[6], (NLAT, NLON), 0, 3) < 1).astype(jnp.int32), jax.random.fold_in(streams_of[6], 1), 0, 1)
    soil_type = touch_ends(jax.random.randint(streams_of[7], (NLAT, NLON), 0, SOIL_TYPES), jax.random.fold_in(streams_of[7], 1), 0, SOIL_TYPES - 1).astype(jnp.int32)
    plant_type = touch_ends(jax.random.randint(streams_of[8], (NLAT, NLON), 0, PLANT_TYPES), jax.random.fold_in(streams_of[8], 1), 0, PLANT_TYPES - 1).astype(jnp.int32)
    soil_params = jnp.clip(jax.random.uniform(streams_of[9], (2, SOIL_TYPES), jnp.float32, 0.0, 1.0), 0.0, 1.0)
    root_profile = jnp.clip(jnp.exp(jax.random.uniform(streams_of[10], (PLANT_TYPES, SOIL_LAYERS), jnp.float32, math.log(0.1), math.log(10.0))), 0.1, 10.0)
    return {"spectra": spectra, "legendre": legendre, "wave_of_slot": wave_of_slot, "row_points": row_points, "row_weight": row_weight, "soil_water": soil_water, "land_mask": land_mask, "soil_type": soil_type, "plant_type": plant_type, "soil_params": soil_params, "root_profile": root_profile}


TWO_PI = 2.0 * math.pi
DEPTHS = (0.07, 0.21, 0.72, 1.89)
UPTAKE_SHARE = 4.0

def wave_tables(wavenumbers, points, longitudes, table_type):
    phases = wavenumbers[:, None] * longitudes[None, :] % points
    angles = phases.astype(jnp.float32) * TWO_PI / points.astype(jnp.float32)
    inside = longitudes[None, :] < points
    cosine_table = jnp.where(inside, jnp.cos(angles), 0.0).astype(table_type)
    sine_table = jnp.where(inside, jnp.sin(angles), 0.0).astype(table_type)
    return (cosine_table, sine_table)

def physics(grid_fields, longitudes, row_points, soil_water, land_mask, soil_type, plant_type, soil_params, root_profile):
    values = grid_fields.astype(jnp.float32)
    wind_u = values[:, LEVELS - 1, :]
    wind_v = values[:, 2 * LEVELS - 1, :]
    air_temp = values[:, 3 * LEVELS - 1, :]
    humidity = values[:, 4 * LEVELS - 1, :]
    skin_temp = values[:, 5 * LEVELS - 1, :]
    wind_speed = jnp.sqrt(1.0 + wind_u * wind_u + wind_v * wind_v)
    demand = 0.5 * wind_speed * jax.nn.softplus(air_temp - humidity)
    in_row = (longitudes[None, :] < row_points[:, None]).astype(jnp.float32)
    usable = in_row * land_mask.astype(jnp.float32)
    soil_onehot = (soil_type[:, :, None] == jnp.arange(SOIL_TYPES, dtype=jnp.int32)).astype(jnp.float32)
    wilting = 0.04 + 0.1 * lax.optimization_barrier(jnp.sum(soil_onehot * soil_params[0], axis=-1))
    capacity = 0.3 + 0.15 * lax.optimization_barrier(jnp.sum(soil_onehot * soil_params[1], axis=-1))
    fractions = root_profile / lax.optimization_barrier(jnp.sum(root_profile, axis=1, keepdims=True))
    plant_onehot = (plant_type[:, :, None] == jnp.arange(PLANT_TYPES, dtype=jnp.int32)).astype(jnp.float32)
    stress = jnp.zeros_like(demand)
    reserve = jnp.zeros_like(demand)
    layer_terms = []
    for layer_num in range(SOIL_LAYERS):
        root_share = lax.optimization_barrier(jnp.sum(plant_onehot * fractions[:, layer_num], axis=-1))
        moisture = soil_water[:, layer_num, :]
        factor = jnp.clip((moisture - wilting) / (capacity - wilting), 0.0, 1.0)
        layer_terms.append(usable * demand * root_share * factor)
        stress = stress + root_share * factor
        reserve = reserve + root_share * DEPTHS[layer_num] * jnp.maximum(moisture - wilting, 0.0)
    transpiration = usable * demand * stress
    available = usable * reserve
    other_fluxes = (in_row * wind_speed * (skin_temp - air_temp), in_row * wind_speed * wind_u, in_row * wind_speed * wind_v)
    return (layer_terms, transpiration, available, other_fluxes)

def reference(spectra, legendre, wave_of_slot, row_points, row_weight, soil_water, land_mask, soil_type, plant_type, soil_params, root_profile):
    offsets = jnp.arange(NJ, dtype=jnp.int32)
    kept_rows = offsets[None, :] < (M - wave_of_slot)[:, None]
    masked = jnp.where(kept_rows[:, :, None], spectra, jnp.zeros_like(spectra))

    def legendre_slot(inputs):
        poly_table, coeff_rows = inputs
        return jnp.dot(poly_table.T, coeff_rows, preferred_element_type=jnp.float32).astype(jnp.bfloat16)
    fourier = lax.map(legendre_slot, (legendre, masked))
    longitudes = jnp.arange(NLON, dtype=jnp.int32)
    synth_scale = 1.0 / math.sqrt(M)

    def synth_row(inputs):
        row_coeffs, points = inputs
        halves = row_coeffs.reshape(M, FL // GROUP, 2, GROUP)
        real_part = halves[:, :, 0, :].reshape(M, FL)
        imag_part = halves[:, :, 1, :].reshape(M, FL)
        cosine_table, sine_table = wave_tables(wave_of_slot, points, longitudes, jnp.bfloat16)
        summed = jnp.dot(real_part.T, cosine_table, preferred_element_type=jnp.float32) - jnp.dot(imag_part.T, sine_table, preferred_element_type=jnp.float32)
        return (summed * synth_scale).astype(jnp.bfloat16)
    grid_fields = lax.map(synth_row, (jnp.transpose(fourier, (1, 0, 2)), row_points))
    layer_terms, transpiration, available, other_fluxes = physics(grid_fields, longitudes, row_points, soil_water, land_mask, soil_type, plant_type, soil_params, root_profile)
    cell_area = (row_weight / row_points.astype(jnp.float32))[:, None]
    demand_total = jnp.sum(cell_area * transpiration)
    avail_total = jnp.sum(cell_area * available)
    fix_ratio = UPTAKE_SHARE * avail_total / demand_total
    uptake = jnp.stack([fix_ratio * layer_term for layer_term in layer_terms], axis=1)
    fluxes = jnp.stack([fix_ratio * transpiration, other_fluxes[0], other_fluxes[1], other_fluxes[2]], axis=1)

    def analyse_row(inputs):
        row_flux, points, weight = inputs
        cosine_table, sine_table = wave_tables(wave_of_slot, points, longitudes, jnp.float32)
        real_part = jnp.dot(row_flux, cosine_table.T, precision=lax.Precision.HIGHEST, preferred_element_type=jnp.float32)
        imag_part = -jnp.dot(row_flux, sine_table.T, precision=lax.Precision.HIGHEST, preferred_element_type=jnp.float32)
        coeffs = jnp.stack([real_part, imag_part], axis=1).reshape(2 * FLUXES, M)
        coeffs = coeffs / jnp.sqrt(points.astype(jnp.float32))
        return (weight * coeffs).astype(jnp.bfloat16)
    weighted = lax.map(analyse_row, (fluxes, row_points, row_weight))

    def analyse_slot(inputs):
        poly_table, column, wavenumber = inputs
        result = jnp.dot(column.T, poly_table.T, preferred_element_type=jnp.float32)
        return jnp.where(offsets[None, :] < M - wavenumber, result, 0.0)
    spectral_fluxes = lax.map(analyse_slot, (legendre, jnp.transpose(weighted, (2, 0, 1)), wave_of_slot))
    return (grid_fields, uptake, spectral_fluxes)
```

```python
import functools
import math

import jax
import jax.numpy as jnp
from jax import lax
from jax.experimental import pallas as pl
from jax.experimental.pallas import tpu as pltpu
from jax.sharding import PartitionSpec as P

LEVELS = 8
FLUXES = 4
SOIL_LAYERS = 4
TWO_PI = 2.0 * math.pi
DEPTHS = (0.07, 0.21, 0.72, 1.89)
UPTAKE_SHARE = 4.0
MESH = pl.DeviceIdType.MESH
HIGHEST = lax.Precision.HIGHEST
SLOT_PAD = 16
CHUNK_WA = 8
CHUNK = SLOT_PAD * CHUNK_WA
LANES = 128


def dot(lhs, rhs, lhs_dim, rhs_dim, precision=None):
    return lax.dot_general(
        lhs,
        rhs,
        (((lhs_dim,), (rhs_dim,)), ((), ())),
        precision=precision,
        preferred_element_type=jnp.float32,
    )


def iota(shape, dim):
    return lax.broadcasted_iota(jnp.int32, shape, dim)


def cos_sin(waves, longitudes, points):
    product = waves * longitudes
    residue = product - points * jnp.round(product * (1.0 / points))
    angle = residue * (TWO_PI / points)
    return jnp.cos(angle), jnp.sin(angle)


def kernel(
    wa_count,
    af_count,
    spectra_ref,
    legendre_ref,
    wave_smem,
    wave_ref,
    points_smem,
    weight_smem,
    water_ref,
    land_ref,
    soil_ref,
    plant_ref,
    params_ref,
    roots_ref,
    grid_ref,
    uptake_ref,
    spectral_ref,
    leg_all,
    placed,
    four_rows,
    four_send,
    four_recv,
    tables,
    coef_send,
    coef_recv,
    send_sems,
    recv_sems,
):
    slots, offsets, cols = spectra_ref.shape
    n_local = legendre_ref.shape[1]
    lat_count = legendre_ref.shape[2]
    waves_total = wave_ref.shape[1]
    lon_count = water_ref.shape[2]
    group = cols // 2
    devices = wa_count * af_count
    chunks = wa_count // CHUNK_WA
    my_wa = lax.axis_index("wa")
    my_af = lax.axis_index("af")
    me = my_wa * af_count + my_af
    my_block = my_af * wa_count + my_wa

    def partner(step):
        other = lax.rem(me + step, devices)
        return lax.div(other, af_count), lax.rem(other, af_count)

    barrier = pltpu.get_barrier_semaphore()

    def greet(step, carry):
        pl.semaphore_signal(barrier, inc=1, device_id=partner(step), device_id_type=MESH)
        return carry

    lax.fori_loop(1, devices, greet, 0)

    place = (
        iota((n_local, offsets), 1) == iota((n_local, offsets), 0) + my_af * n_local
    ).astype(jnp.float32).astype(jnp.bfloat16)
    lane_offset = iota((lat_count, offsets), 1)
    parts = []
    for s in range(slots):
        turned = dot(legendre_ref[s], place, 0, 0)
        kept = lane_offset < waves_total - wave_smem[my_wa * slots + s]
        parts.append(jnp.where(kept, turned, 0.0))
    leg_all[my_af] = jnp.concatenate(parts, axis=0).astype(jnp.bfloat16)

    pl.semaphore_wait(barrier, devices - 1)

    def send_legendre(step, carry):
        pltpu.make_async_remote_copy(
            src_ref=leg_all.at[my_af],
            dst_ref=leg_all.at[my_af],
            send_sem=send_sems.at[0],
            recv_sem=recv_sems.at[0],
            device_id=(my_wa, lax.rem(my_af + step, af_count)),
            device_id_type=MESH,
        ).start()
        return carry

    lax.fori_loop(1, af_count, send_legendre, 0)

    col_place = (
        iota((cols, LANES), 1) == iota((cols, LANES), 0) + my_af * cols
    ).astype(jnp.float32).astype(jnp.bfloat16)
    for s in range(slots):
        placed[s] = dot(spectra_ref[s], col_place, 1, 0).astype(jnp.bfloat16)
    four_rows[...] = jnp.zeros_like(four_rows)

    leg_bytes = leg_all.at[pl.ds(0, af_count - 1)]
    pltpu.make_async_copy(leg_bytes, leg_bytes, recv_sems.at[0]).wait()

    for s in range(slots):
        rows = pl.ds(s * lat_count, lat_count)
        full = leg_all[0, rows, :].astype(jnp.float32)
        for other in range(1, af_count):
            full = full + leg_all[other, rows, :].astype(jnp.float32)
        four_rows[pl.ds(s, lat_count, stride=SLOT_PAD), :] = dot(
            full.astype(jnp.bfloat16), placed[s], 1, 0
        )
    four_send[...] = four_rows[...].astype(jnp.bfloat16).reshape(four_send.shape)

    def send_fourier(step, carry):
        to_wa, to_af = partner(step)
        pltpu.make_async_remote_copy(
            src_ref=four_send.at[to_wa],
            dst_ref=four_recv.at[my_block],
            send_sem=send_sems.at[1],
            recv_sem=recv_sems.at[1],
            device_id=(to_wa, to_af),
            device_id_type=MESH,
        ).start()
        return carry

    lax.fori_loop(1, devices, send_fourier, 0)
    four_recv[my_block] = four_send[my_wa]

    points_int = points_smem[0]
    points = points_int.astype(jnp.float32)
    points_vec = jnp.full((1, 1), points, jnp.float32)
    first_lon = my_af * lon_count
    waves_row = wave_ref[...].astype(jnp.float32)

    def fill_tables(chunk, carry):
        row = iota((CHUNK, waves_total), 0)
        slot = lax.rem(row, SLOT_PAD)
        named = iota((CHUNK, waves_total), 1) == (
            (lax.div(row, SLOT_PAD) + chunk * CHUNK_WA) * slots + slot
        )
        named = jnp.logical_and(named, slot < slots)
        waves = jnp.sum(jnp.where(named, waves_row, 0.0), axis=1, keepdims=True)
        lane = iota((1, LANES), 1)
        base_cos, base_sin = cos_sin(waves, lane.astype(jnp.float32), points_vec)
        starts = (first_lon + LANES * lane).astype(jnp.float32)
        start_cos, start_sin = cos_sin(waves, starts, points_vec)
        for block in range(lon_count // LANES):
            part = pl.ds(block * LANES, LANES)
            c0 = start_cos[:, block : block + 1]
            s0 = start_sin[:, block : block + 1]
            tables[chunk, pl.ds(0, CHUNK), part] = (base_cos * c0 - base_sin * s0).astype(
                jnp.bfloat16
            )
            tables[chunk, pl.ds(CHUNK, CHUNK), part] = (
                -(base_sin * c0) - base_cos * s0
            ).astype(jnp.bfloat16)
        return carry

    if chunks == 1:
        fill_tables(0, 0)
    else:
        lax.fori_loop(0, chunks, fill_tables, 0)

    longitudes = first_lon + iota((1, lon_count), 1)
    in_row = (longitudes < points_int).astype(jnp.float32)
    usable = in_row * land_ref[...].astype(jnp.float32)
    soil_kinds = params_ref.shape[1]
    plant_kinds = roots_ref.shape[0]
    soil_hot = (iota((soil_kinds, lon_count), 0) == soil_ref[...]).astype(jnp.float32)
    plant_hot = (iota((plant_kinds, lon_count), 0) == plant_ref[...]).astype(jnp.float32)
    soil = dot(params_ref[...], soil_hot, 1, 0, HIGHEST)
    wilting = 0.04 + 0.1 * soil[0:1]
    capacity = 0.3 + 0.15 * soil[1:2]
    roots = roots_ref[...]
    fractions = roots / jnp.sum(roots, axis=1, keepdims=True)
    root_share = dot(fractions, plant_hot, 0, 0, HIGHEST)
    moisture = water_ref[0]
    excess = moisture - wilting
    factor = jnp.clip(excess / (capacity - wilting), 0.0, 1.0)
    share_factor = root_share * factor
    stress = jnp.sum(share_factor, axis=0, keepdims=True)
    layer = iota((SOIL_LAYERS, 1), 0)
    depths = jnp.full((SOIL_LAYERS, 1), DEPTHS[0], jnp.float32)
    for number in range(1, SOIL_LAYERS):
        depths = jnp.where(layer == number, DEPTHS[number], depths)
    reserve = jnp.sum(root_share * depths * jnp.maximum(excess, 0.0), axis=0, keepdims=True)
    available = usable * reserve

    four_bytes = four_recv.at[pl.ds(0, devices - 1)]
    pltpu.make_async_copy(four_bytes, four_bytes, recv_sems.at[1]).wait()

    def synthesize(chunk, total):
        summed = jnp.zeros((CHUNK, LANES), jnp.float32)
        for other in range(af_count):
            got = four_recv[pl.ds(other * wa_count + chunk * CHUNK_WA, CHUNK_WA)]
            summed = summed + got.reshape(CHUNK, LANES).astype(jnp.float32)
        turned = summed.T
        real = [turned[cols * g : cols * g + group] for g in range(af_count)]
        imag = [turned[cols * g + group : cols * (g + 1)] for g in range(af_count)]
        both = jnp.concatenate(
            [jnp.concatenate(real, axis=0), jnp.concatenate(imag, axis=0)], axis=1
        ).astype(jnp.bfloat16)
        return total + dot(both, tables[chunk], 1, 0)

    fields = jnp.zeros((group * af_count, lon_count), jnp.float32)
    if chunks == 1:
        fields = synthesize(0, fields)
    else:
        fields = lax.fori_loop(0, chunks, synthesize, fields)
    rounded = (fields * in_row * (1.0 / math.sqrt(waves_total))).astype(jnp.bfloat16)
    grid_ref[0] = rounded
    values = rounded.astype(jnp.float32)

    def lowest(field):
        return values[(field + 1) * LEVELS - 1 : (field + 1) * LEVELS]

    wind_u, wind_v, air, humid, skin = [lowest(f) for f in range(5)]
    speed = jnp.sqrt(1.0 + wind_u * wind_u + wind_v * wind_v)
    gap = air - humid
    softplus = jnp.maximum(gap, 0.0) + jnp.log1p(jnp.exp(-jnp.abs(gap)))
    demand = usable * (0.5 * speed * softplus)
    transpiration = demand * stress
    moving = in_row * speed
    fluxes = (transpiration, moving * (skin - air), moving * wind_u, moving * wind_v)
    nothing = jnp.zeros_like(demand)
    even, odd = [], []
    for flux in fluxes:
        even += [flux, nothing]
        odd += [nothing, flux]
    even = jnp.concatenate(even, axis=0)
    odd = jnp.concatenate(odd, axis=0)
    even = jnp.concatenate([even] * SLOT_PAD, axis=0).astype(jnp.bfloat16)
    odd = jnp.concatenate([odd] * SLOT_PAD, axis=0).astype(jnp.bfloat16)
    weight = weight_smem[0]
    area = weight / points_vec
    transpired = jnp.sum(transpiration, axis=1, keepdims=True) * area
    reserved = jnp.sum(available, axis=1, keepdims=True) * area
    row_scale = weight * lax.rsqrt(points_vec)

    rows8 = 2 * FLUXES
    first_spare = slots * rows8

    def analyse(chunk, carry):
        product = dot(tables[chunk, pl.ds(0, CHUNK), :], even, 1, 1) + dot(
            tables[chunk, pl.ds(CHUNK, CHUNK), :], odd, 1, 1
        )
        slot = lax.rem(iota((CHUNK, LANES), 0), SLOT_PAD)
        lane = iota((CHUNK, LANES), 1)
        mine = jnp.logical_and(lax.div(lane, rows8) == slot, slot < slots)
        kept = jnp.where(mine, product, 0.0).reshape(CHUNK_WA, SLOT_PAD, LANES)
        line = jnp.sum(kept, axis=1) * row_scale
        lane = iota((CHUNK_WA, LANES), 1)
        line = jnp.where(lane == first_spare, transpired, line)
        line = jnp.where(lane == first_spare + 1, reserved, line)
        coef_send[pl.ds(chunk * CHUNK_WA, CHUNK_WA)] = line.reshape(CHUNK_WA, 1, LANES)
        return carry

    if chunks == 1:
        analyse(0, 0)
    else:
        lax.fori_loop(0, chunks, analyse, 0)

    def send_coeffs(step, carry):
        to_wa, to_af = partner(step)
        pltpu.make_async_remote_copy(
            src_ref=coef_send.at[to_wa],
            dst_ref=coef_recv.at[my_block],
            send_sem=send_sems.at[2],
            recv_sem=recv_sems.at[2],
            device_id=(to_wa, to_af),
            device_id_type=MESH,
        ).start()
        return carry

    lax.fori_loop(1, devices, send_coeffs, 0)
    coef_recv[my_block] = coef_send[my_wa]
    unfixed = demand * share_factor
    pltpu.make_async_copy(leg_bytes, leg_bytes, send_sems.at[0]).wait()
    pltpu.make_async_copy(four_bytes, four_bytes, send_sems.at[1]).wait()

    coef_bytes = coef_recv.at[pl.ds(0, devices - 1)]
    pltpu.make_async_copy(coef_bytes, coef_bytes, recv_sems.at[2]).wait()

    lines = coef_recv[pl.ds(0, wa_count)]
    for other in range(1, af_count):
        lines = lines + coef_recv[pl.ds(other * wa_count, wa_count)]
    lines = lines.reshape(wa_count, LANES)
    totals = jnp.sum(lines, axis=0, keepdims=True)
    fix_ratio = UPTAKE_SHARE * totals[:, first_spare + 1 : first_spare + 2] / (
        totals[:, first_spare : first_spare + 1]
    )
    uptake_ref[0] = fix_ratio * unfixed
    scaled = jnp.where(lax.rem(iota((1, LANES), 1), rows8) < 2, fix_ratio, 1.0) * lines
    turned = scaled.T
    offset = iota((rows8, n_local), 1) + my_af * n_local
    for s in range(slots):
        weighted = turned[s * rows8 : (s + 1) * rows8].astype(jnp.bfloat16)
        result = dot(weighted, legendre_ref[s], 1, 1)
        kept = offset < waves_total - wave_smem[my_wa * slots + s]
        spectral_ref[s] = jnp.where(kept, result, 0.0)

    pltpu.make_async_copy(coef_bytes, coef_bytes, send_sems.at[2]).wait()


def per_device(
    spectra,
    legendre,
    wave_of_slot,
    row_points,
    row_weight,
    soil_water,
    land_mask,
    soil_type,
    plant_type,
    soil_params,
    root_profile,
):
    wa_count = lax.axis_size("wa")
    af_count = lax.axis_size("af")
    slots, offsets, cols = spectra.shape
    n_local, lat_count = legendre.shape[1:]
    waves_total = wave_of_slot.shape[0]
    lon_count = soil_water.shape[2]
    devices = wa_count * af_count
    chunks = wa_count // CHUNK_WA
    assert row_points.shape[0] == 1 and lat_count == wa_count and cols * af_count == LANES
    assert slots * 2 * FLUXES + 2 <= LANES and slots <= SLOT_PAD
    assert wa_count % CHUNK_WA == 0 and lon_count % LANES == 0
    vmem = pl.BlockSpec(memory_space=pltpu.VMEM)
    smem = pl.BlockSpec(memory_space=pltpu.SMEM)
    return pl.pallas_call(
        functools.partial(kernel, wa_count, af_count),
        out_shape=(
            jax.ShapeDtypeStruct((1, cols // 2 * af_count, lon_count), jnp.bfloat16),
            jax.ShapeDtypeStruct((1, SOIL_LAYERS, lon_count), jnp.float32),
            jax.ShapeDtypeStruct((slots, 2 * FLUXES, n_local), jnp.float32),
        ),
        in_specs=[vmem, vmem, smem, vmem, smem, smem] + [vmem] * 6,
        out_specs=(vmem, vmem, vmem),
        scratch_shapes=[
            pltpu.VMEM((af_count, slots * lat_count, offsets), jnp.bfloat16),
            pltpu.VMEM((slots, offsets, LANES), jnp.bfloat16),
            pltpu.VMEM((lat_count * SLOT_PAD, LANES), jnp.float32),
            pltpu.VMEM((lat_count, SLOT_PAD, LANES), jnp.bfloat16),
            pltpu.VMEM((devices, SLOT_PAD, LANES), jnp.bfloat16),
            pltpu.VMEM((chunks, 2 * CHUNK, lon_count), jnp.bfloat16),
            pltpu.VMEM((wa_count, 1, LANES), jnp.float32),
            pltpu.VMEM((devices, 1, LANES), jnp.float32),
            pltpu.SemaphoreType.DMA((3,)),
            pltpu.SemaphoreType.DMA((3,)),
        ],
        compiler_params=pltpu.CompilerParams(
            collective_id=0,
            has_side_effects=True,
            vmem_limit_bytes=(48 if chunks > 1 else 16) * 1024 * 1024,
        ),
    )(
        spectra,
        legendre,
        wave_of_slot,
        wave_of_slot.reshape(1, waves_total),
        row_points,
        row_weight,
        soil_water,
        land_mask,
        soil_type,
        plant_type,
        soil_params,
        root_profile,
    )


def solution(mesh):
    in_specs = (
        P("wa", None, "af"),
        P("wa", "af", None),
        P(),
        P("wa"),
        P("wa"),
        P("wa", None, "af"),
        P("wa", "af"),
        P("wa", "af"),
        P("wa", "af"),
        P(),
        P(),
    )
    out_specs = (P("wa", None, "af"), P("wa", None, "af"), P("wa", None, "af"))
    return jax.shard_map(
        per_device, mesh=mesh, in_specs=in_specs, out_specs=out_specs, check_vma=False
    )
```

```python
import functools
import math

import jax
import jax.numpy as jnp
from jax import lax
from jax.experimental import pallas as pl
from jax.experimental.pallas import tpu as pltpu
from jax.sharding import PartitionSpec as P

LEVELS = 8
FLUXES = 4
SOIL_LAYERS = 4
TWO_PI = 2.0 * math.pi
DEPTHS = (0.07, 0.21, 0.72, 1.89)
UPTAKE_SHARE = 4.0
MESH = pl.DeviceIdType.MESH
HIGHEST = lax.Precision.HIGHEST
SLOT_PAD = 16
CHUNK_WA = 8
CHUNK = SLOT_PAD * CHUNK_WA
LANES = 128


def dot(lhs, rhs, lhs_dim, rhs_dim, precision=None):
    return lax.dot_general(
        lhs,
        rhs,
        (((lhs_dim,), (rhs_dim,)), ((), ())),
        precision=precision,
        preferred_element_type=jnp.float32,
    )


def iota(shape, dim):
    return lax.broadcasted_iota(jnp.int32, shape, dim)


def cos_sin(waves, longitudes, points):
    product = waves * longitudes
    residue = product - points * jnp.round(product * (1.0 / points))
    quarters = residue * (4.0 / points)
    quadrant = jnp.round(quarters)
    angle = (quarters - quadrant) * (0.25 * TWO_PI)
    square = angle * angle
    cosine = 1.0 + square * (
        -1 / 2 + square * (1 / 24 + square * (-1 / 720 + square * (1 / 40320)))
    )
    sine = angle * (
        1.0 + square * (-1 / 6 + square * (1 / 120 + square * (-1 / 5040 + square * (1 / 362880))))
    )
    size = jnp.abs(quadrant)
    odd = size == 1.0
    sign = 1.0 - size
    return (
        jnp.where(odd, -quadrant * sine, sign * cosine),
        jnp.where(odd, quadrant * cosine, sign * sine),
    )


def kernel(
    wa_count,
    af_count,
    spectra_ref,
    legendre_ref,
    wave_smem,
    wave_ref,
    points_smem,
    weight_smem,
    water_ref,
    land_ref,
    soil_ref,
    plant_ref,
    params_ref,
    roots_ref,
    grid_ref,
    uptake_ref,
    spectral_ref,
    leg_all,
    placed,
    four_rows,
    four_send,
    four_recv,
    tables,
    coef_send,
    coef_recv,
    send_sems,
    recv_sems,
):
    slots, cols, offsets = spectra_ref.shape
    lat_count = legendre_ref.shape[1]
    n_local = legendre_ref.shape[2]
    waves_total = wave_ref.shape[1]
    lon_count = water_ref.shape[2]
    group = cols // 2
    devices = wa_count * af_count
    chunks = wa_count // CHUNK_WA
    my_wa = lax.axis_index("wa")
    my_af = lax.axis_index("af")
    my_block = my_af * wa_count + my_wa

    def wrapped(index, count):
        return jnp.where(index >= count, index - count, index)

    af_peers = [my_af] + [wrapped(my_af + step, af_count) for step in range(1, af_count)]

    def each_partner(act):
        def row(step, carry):
            to_wa = wrapped(my_wa + step, wa_count)
            for to_af in af_peers:
                act(to_wa, to_af)
            return carry

        lax.fori_loop(1, wa_count, row, 0)
        for to_af in af_peers[1:]:
            act(my_wa, to_af)

    barrier = pltpu.get_barrier_semaphore()

    def greet(to_wa, to_af):
        pl.semaphore_signal(barrier, inc=1, device_id=(to_wa, to_af), device_id_type=MESH)

    each_partner(greet)

    place = (
        iota((n_local, offsets), 1) == iota((n_local, offsets), 0) + my_af * n_local
    ).astype(jnp.float32).astype(jnp.bfloat16)
    lane_offset = iota((lat_count, offsets), 1)
    parts = []
    for s in range(slots):
        turned = dot(legendre_ref[s], place, 1, 0)
        kept = lane_offset < waves_total - wave_smem[my_wa * slots + s]
        parts.append(jnp.where(kept, turned, 0.0))
    leg_all[my_af] = jnp.concatenate(parts, axis=0).astype(jnp.bfloat16)

    pl.semaphore_wait(barrier, devices - 1)

    for to_af in af_peers[1:]:
        pltpu.make_async_remote_copy(
            src_ref=leg_all.at[my_af],
            dst_ref=leg_all.at[my_af],
            send_sem=send_sems.at[0],
            recv_sem=recv_sems.at[0],
            device_id=(my_wa, to_af),
            device_id_type=MESH,
        ).start()

    placed[...] = jnp.zeros_like(placed)
    for s in range(slots):
        placed[s, pl.ds(pl.multiple_of(my_af * cols, cols), cols), :] = spectra_ref[s]
    four_rows[...] = jnp.zeros_like(four_rows)

    points_int = points_smem[0]
    points = points_int.astype(jnp.float32)
    points_vec = jnp.full((1, 1), points, jnp.float32)
    first_lon = my_af * lon_count
    waves_row = wave_ref[...].astype(jnp.float32)

    def fill_tables(chunk, carry):
        row = iota((CHUNK, waves_total), 0)
        slot = lax.rem(row, SLOT_PAD)
        named = iota((CHUNK, waves_total), 1) == (
            (lax.div(row, SLOT_PAD) + chunk * CHUNK_WA) * slots + slot
        )
        named = jnp.logical_and(named, slot < slots)
        waves = jnp.sum(jnp.where(named, waves_row, 0.0), axis=1, keepdims=True)
        lane = iota((1, LANES), 1)
        base_cos, base_sin = cos_sin(waves, lane.astype(jnp.float32), points_vec)
        starts = (first_lon + LANES * lane).astype(jnp.float32)
        start_cos, start_sin = cos_sin(waves, starts, points_vec)
        for block in range(lon_count // LANES):
            part = pl.ds(block * LANES, LANES)
            c0 = start_cos[:, block : block + 1]
            s0 = start_sin[:, block : block + 1]
            tables[chunk, pl.ds(0, CHUNK), part] = (base_cos * c0 - base_sin * s0).astype(
                jnp.bfloat16
            )
            tables[chunk, pl.ds(CHUNK, CHUNK), part] = (
                -(base_sin * c0) - base_cos * s0
            ).astype(jnp.bfloat16)
        return carry

    if chunks == 1:
        fill_tables(0, 0)
    else:
        lax.fori_loop(0, chunks, fill_tables, 0)

    leg_bytes = leg_all.at[pl.ds(0, af_count - 1)]
    pltpu.make_async_copy(leg_bytes, leg_bytes, recv_sems.at[0]).wait()

    for s in range(slots):
        rows = pl.ds(s * lat_count, lat_count)
        full = leg_all[0, rows, :].astype(jnp.float32)
        for other in range(1, af_count):
            full = full + leg_all[other, rows, :].astype(jnp.float32)
        four_rows[pl.ds(s, lat_count, stride=SLOT_PAD), :] = dot(
            full.astype(jnp.bfloat16), placed[s], 1, 1
        )
    four_send[...] = four_rows[...].astype(jnp.bfloat16).reshape(four_send.shape)

    def send_fourier(to_wa, to_af):
        pltpu.make_async_remote_copy(
            src_ref=four_send.at[to_wa],
            dst_ref=four_recv.at[my_block],
            send_sem=send_sems.at[1],
            recv_sem=recv_sems.at[1],
            device_id=(to_wa, to_af),
            device_id_type=MESH,
        ).start()

    each_partner(send_fourier)
    four_recv[my_block] = four_send[my_wa]

    longitudes = first_lon + iota((1, lon_count), 1)
    in_row = (longitudes < points_int).astype(jnp.float32)
    usable = in_row * land_ref[...].astype(jnp.float32)
    soil_kinds = params_ref.shape[1]
    plant_kinds = roots_ref.shape[1]
    soil_hot = (iota((soil_kinds, lon_count), 0) == soil_ref[...]).astype(jnp.float32)
    plant_hot = (iota((plant_kinds, lon_count), 0) == plant_ref[...]).astype(jnp.float32)
    soil = dot(params_ref[...], soil_hot, 1, 0, HIGHEST)
    wilting = 0.04 + 0.1 * soil[0:1]
    capacity = 0.3 + 0.15 * soil[1:2]
    roots = roots_ref[...]
    fractions = roots / jnp.sum(roots, axis=0, keepdims=True)
    root_share = dot(fractions, plant_hot, 1, 0, HIGHEST)
    moisture = water_ref[0]
    excess = moisture - wilting
    factor = jnp.clip(excess / (capacity - wilting), 0.0, 1.0)
    share_factor = root_share * factor
    stress = jnp.sum(share_factor, axis=0, keepdims=True)
    layer = iota((SOIL_LAYERS, 1), 0)
    depths = jnp.full((SOIL_LAYERS, 1), DEPTHS[0], jnp.float32)
    for number in range(1, SOIL_LAYERS):
        depths = jnp.where(layer == number, DEPTHS[number], depths)
    reserve = jnp.sum(root_share * depths * jnp.maximum(excess, 0.0), axis=0, keepdims=True)
    available = usable * reserve

    four_bytes = four_recv.at[pl.ds(0, devices - 1)]
    pltpu.make_async_copy(four_bytes, four_bytes, recv_sems.at[1]).wait()

    def synthesize(chunk, total):
        summed = jnp.zeros((CHUNK, LANES), jnp.float32)
        for other in range(af_count):
            got = four_recv[pl.ds(other * wa_count + chunk * CHUNK_WA, CHUNK_WA)]
            summed = summed + got.reshape(CHUNK, LANES).astype(jnp.float32)
        turned = summed.T
        real = [turned[cols * g : cols * g + group] for g in range(af_count)]
        imag = [turned[cols * g + group : cols * (g + 1)] for g in range(af_count)]
        both = jnp.concatenate(
            [jnp.concatenate(real, axis=0), jnp.concatenate(imag, axis=0)], axis=1
        ).astype(jnp.bfloat16)
        return total + dot(both, tables[chunk], 1, 0)

    fields = jnp.zeros((group * af_count, lon_count), jnp.float32)
    if chunks == 1:
        fields = synthesize(0, fields)
    else:
        fields = lax.fori_loop(0, chunks, synthesize, fields)
    rounded = (fields * in_row * (1.0 / math.sqrt(waves_total))).astype(jnp.bfloat16)
    grid_ref[0] = rounded
    values = rounded.astype(jnp.float32)

    def lowest(field):
        return values[(field + 1) * LEVELS - 1 : (field + 1) * LEVELS]

    wind_u, wind_v, air, humid, skin = [lowest(f) for f in range(5)]
    speed = jnp.sqrt(1.0 + wind_u * wind_u + wind_v * wind_v)
    gap = air - humid
    softplus = jnp.maximum(gap, 0.0) + jnp.log1p(jnp.exp(-jnp.abs(gap)))
    demand = usable * (0.5 * speed * softplus)
    transpiration = demand * stress
    moving = in_row * speed
    fluxes = (transpiration, moving * (skin - air), moving * wind_u, moving * wind_v)
    nothing = jnp.zeros_like(demand)
    even, odd = [], []
    for flux in fluxes:
        even += [flux, nothing]
        odd += [nothing, flux]
    even = jnp.concatenate(even, axis=0)
    odd = jnp.concatenate(odd, axis=0)
    even = jnp.concatenate([even] * SLOT_PAD, axis=0).astype(jnp.bfloat16)
    odd = jnp.concatenate([odd] * SLOT_PAD, axis=0).astype(jnp.bfloat16)
    weight = weight_smem[0]
    area = weight / points_vec
    transpired = jnp.sum(transpiration, axis=1, keepdims=True) * area
    reserved = jnp.sum(available, axis=1, keepdims=True) * area
    row_scale = weight * lax.rsqrt(points_vec)

    rows8 = 2 * FLUXES
    first_spare = slots * rows8

    def analyse(chunk, carry):
        product = dot(tables[chunk, pl.ds(0, CHUNK), :], even, 1, 1) + dot(
            tables[chunk, pl.ds(CHUNK, CHUNK), :], odd, 1, 1
        )
        slot = lax.rem(iota((CHUNK, LANES), 0), SLOT_PAD)
        lane = iota((CHUNK, LANES), 1)
        mine = jnp.logical_and(lax.div(lane, rows8) == slot, slot < slots)
        kept = jnp.where(mine, product, 0.0).reshape(CHUNK_WA, SLOT_PAD, LANES)
        line = jnp.sum(kept, axis=1) * row_scale
        lane = iota((CHUNK_WA, LANES), 1)
        line = jnp.where(lane == first_spare, transpired, line)
        line = jnp.where(lane == first_spare + 1, reserved, line)
        coef_send[pl.ds(chunk * CHUNK_WA, CHUNK_WA)] = line.reshape(CHUNK_WA, 1, LANES)
        return carry

    if chunks == 1:
        analyse(0, 0)
    else:
        lax.fori_loop(0, chunks, analyse, 0)

    def send_coeffs(to_wa, to_af):
        pltpu.make_async_remote_copy(
            src_ref=coef_send.at[to_wa],
            dst_ref=coef_recv.at[my_block],
            send_sem=send_sems.at[2],
            recv_sem=recv_sems.at[2],
            device_id=(to_wa, to_af),
            device_id_type=MESH,
        ).start()

    each_partner(send_coeffs)
    coef_recv[my_block] = coef_send[my_wa]
    unfixed = demand * share_factor
    pltpu.make_async_copy(leg_bytes, leg_bytes, send_sems.at[0]).wait()
    pltpu.make_async_copy(four_bytes, four_bytes, send_sems.at[1]).wait()

    coef_bytes = coef_recv.at[pl.ds(0, devices - 1)]
    pltpu.make_async_copy(coef_bytes, coef_bytes, recv_sems.at[2]).wait()

    lines = coef_recv[pl.ds(0, wa_count)]
    for other in range(1, af_count):
        lines = lines + coef_recv[pl.ds(other * wa_count, wa_count)]
    lines = lines.reshape(wa_count, LANES)
    totals = jnp.sum(lines, axis=0, keepdims=True)
    fix_ratio = UPTAKE_SHARE * totals[:, first_spare + 1 : first_spare + 2] / (
        totals[:, first_spare : first_spare + 1]
    )
    uptake_ref[0] = fix_ratio * unfixed
    scaled = jnp.where(lax.rem(iota((1, LANES), 1), rows8) < 2, fix_ratio, 1.0) * lines
    turned = scaled.T
    offset = iota((rows8, n_local), 1) + my_af * n_local
    for s in range(slots):
        weighted = turned[s * rows8 : (s + 1) * rows8].astype(jnp.bfloat16)
        result = dot(weighted, legendre_ref[s], 1, 0)
        kept = offset < waves_total - wave_smem[my_wa * slots + s]
        spectral_ref[s] = jnp.where(kept, result, 0.0)

    pltpu.make_async_copy(coef_bytes, coef_bytes, send_sems.at[2]).wait()


def per_device(
    spectra,
    legendre,
    wave_of_slot,
    row_points,
    row_weight,
    soil_water,
    land_mask,
    soil_type,
    plant_type,
    soil_params,
    root_profile,
):
    wa_count = lax.axis_size("wa")
    af_count = lax.axis_size("af")
    slots, offsets, cols = spectra.shape
    n_local, lat_count = legendre.shape[1:]
    waves_total = wave_of_slot.shape[0]
    lon_count = soil_water.shape[2]
    devices = wa_count * af_count
    chunks = wa_count // CHUNK_WA
    assert row_points.shape[0] == 1 and lat_count == wa_count and cols * af_count == LANES
    assert slots * 2 * FLUXES + 2 <= LANES and slots <= SLOT_PAD
    assert wa_count % CHUNK_WA == 0 and lon_count % LANES == 0
    vmem = pl.BlockSpec(memory_space=pltpu.VMEM)
    smem = pl.BlockSpec(memory_space=pltpu.SMEM)
    return pl.pallas_call(
        functools.partial(kernel, wa_count, af_count),
        out_shape=(
            jax.ShapeDtypeStruct((1, cols // 2 * af_count, lon_count), jnp.bfloat16),
            jax.ShapeDtypeStruct((1, SOIL_LAYERS, lon_count), jnp.float32),
            jax.ShapeDtypeStruct((slots, 2 * FLUXES, n_local), jnp.float32),
        ),
        in_specs=[vmem, vmem, smem, vmem, smem, smem] + [vmem] * 6,
        out_specs=(vmem, vmem, vmem),
        scratch_shapes=[
            pltpu.VMEM((af_count, slots * lat_count, offsets), jnp.bfloat16),
            pltpu.VMEM((slots, LANES, offsets), jnp.bfloat16),
            pltpu.VMEM((lat_count * SLOT_PAD, LANES), jnp.float32),
            pltpu.VMEM((lat_count, SLOT_PAD, LANES), jnp.bfloat16),
            pltpu.VMEM((devices, SLOT_PAD, LANES), jnp.bfloat16),
            pltpu.VMEM((chunks, 2 * CHUNK, lon_count), jnp.bfloat16),
            pltpu.VMEM((wa_count, 1, LANES), jnp.float32),
            pltpu.VMEM((devices, 1, LANES), jnp.float32),
            pltpu.SemaphoreType.DMA((3,)),
            pltpu.SemaphoreType.DMA((3,)),
        ],
        compiler_params=pltpu.CompilerParams(
            collective_id=0,
            has_side_effects=True,
            vmem_limit_bytes=(48 if chunks > 1 else 16) * 1024 * 1024,
        ),
    )(
        spectra.transpose(0, 2, 1),
        legendre.transpose(0, 2, 1),
        wave_of_slot,
        wave_of_slot.reshape(1, waves_total),
        row_points,
        row_weight,
        soil_water,
        land_mask,
        soil_type,
        plant_type,
        soil_params,
        root_profile.T,
    )


def solution(mesh):
    in_specs = (
        P("wa", None, "af"),
        P("wa", "af", None),
        P(),
        P("wa"),
        P("wa"),
        P("wa", None, "af"),
        P("wa", "af"),
        P("wa", "af"),
        P("wa", "af"),
        P(),
        P(),
    )
    out_specs = (P("wa", None, "af"), P("wa", None, "af"), P("wa", None, "af"))
    return jax.shard_map(
        per_device, mesh=mesh, in_specs=in_specs, out_specs=out_specs, check_vma=False
    )
```

```python
import functools
import math

import jax
import jax.numpy as jnp
from jax import lax
from jax.experimental import pallas as pl
from jax.experimental.pallas import tpu as pltpu
from jax.sharding import PartitionSpec as P

LEVELS = 8
FLUXES = 4
SOIL_LAYERS = 4
TWO_PI = 2.0 * math.pi
DEPTHS = (0.07, 0.21, 0.72, 1.89)
UPTAKE_SHARE = 4.0
MESH = pl.DeviceIdType.MESH
HIGHEST = lax.Precision.HIGHEST
SLOT_PAD = 16
CHUNK_WA = 8
CHUNK = SLOT_PAD * CHUNK_WA
LANES = 128
VMEM_LIMIT = 56 * 1024 * 1024


def dot(lhs, rhs, lhs_dim, rhs_dim, precision=None):
    return lax.dot_general(
        lhs,
        rhs,
        (((lhs_dim,), (rhs_dim,)), ((), ())),
        precision=precision,
        preferred_element_type=jnp.float32,
    )


def iota(shape, dim):
    return lax.broadcasted_iota(jnp.int32, shape, dim)


def cos_sin(waves, longitudes, points):
    product = waves * longitudes
    residue = product - points * jnp.round(product * (1.0 / points))
    quarters = residue * (4.0 / points)
    quadrant = jnp.round(quarters)
    angle = (quarters - quadrant) * (0.25 * TWO_PI)
    square = angle * angle
    cosine = 1.0 + square * (
        -1 / 2 + square * (1 / 24 + square * (-1 / 720 + square * (1 / 40320)))
    )
    sine = angle * (
        1.0 + square * (-1 / 6 + square * (1 / 120 + square * (-1 / 5040 + square * (1 / 362880))))
    )
    size = jnp.abs(quadrant)
    odd = size == 1.0
    sign = 1.0 - size
    return (
        jnp.where(odd, -quadrant * sine, sign * cosine),
        jnp.where(odd, quadrant * cosine, sign * sine),
    )


def kernel(
    wa_count,
    af_count,
    wave_smem,
    points_smem,
    weight_smem,
    legendre_hbm,
    spectra_hbm,
    wave_hbm,
    water_hbm,
    land_hbm,
    soil_hbm,
    plant_hbm,
    params_hbm,
    roots_hbm,
    grid_hbm,
    uptake_ref,
    spectral_ref,
    leg_all,
    placed,
    four_rows,
    four_send,
    four_recv,
    tables,
    coef_send,
    coef_recv,
    legendre_ref,
    spectra_ref,
    wave_ref,
    water_ref,
    land_ref,
    soil_ref,
    plant_ref,
    params_ref,
    roots_ref,
    grid_ref,
    send_sems,
    recv_sems,
    load_sems,
):
    slots, cols, offsets = spectra_ref.shape
    lat_count = legendre_ref.shape[1]
    n_local = legendre_ref.shape[2]
    waves_total = wave_ref.shape[1]
    lon_count = water_ref.shape[2]
    group = cols // 2
    devices = wa_count * af_count
    chunks = wa_count // CHUNK_WA
    my_wa = lax.axis_index("wa")
    my_af = lax.axis_index("af")
    my_block = my_af * wa_count + my_wa

    def wrapped(index, count):
        return jnp.where(index >= count, index - count, index)

    af_peers = [my_af] + [wrapped(my_af + step, af_count) for step in range(1, af_count)]

    def each_partner(act):
        def row(step, carry):
            to_wa = wrapped(my_wa + step, wa_count)
            for to_af in af_peers:
                act(to_wa, to_af)
            return carry

        lax.fori_loop(1, wa_count, row, 0)
        for to_af in af_peers[1:]:
            act(my_wa, to_af)

    barrier = pltpu.get_barrier_semaphore()

    def greet(to_wa, to_af):
        pl.semaphore_signal(barrier, inc=1, device_id=(to_wa, to_af), device_id_type=MESH)

    loads = [
        pltpu.make_async_copy(source, target, load_sems.at[number])
        for number, (source, target) in enumerate(
            (
                (legendre_hbm, legendre_ref),
                (spectra_hbm, spectra_ref),
                (wave_hbm, wave_ref),
                (water_hbm, water_ref),
                (land_hbm, land_ref),
                (soil_hbm, soil_ref),
                (plant_hbm, plant_ref),
                (params_hbm, params_ref),
                (roots_hbm, roots_ref),
            )
        )
    ]
    loads[0].start()
    each_partner(greet)
    for load in loads[1:]:
        load.start()
    loads[0].wait()

    place = (
        iota((n_local, offsets), 1) == iota((n_local, offsets), 0) + my_af * n_local
    ).astype(jnp.float32).astype(jnp.bfloat16)
    lane_offset = iota((lat_count, offsets), 1)
    parts = []
    for s in range(slots):
        turned = dot(legendre_ref[s], place, 1, 0)
        kept = lane_offset < waves_total - wave_smem[my_wa * slots + s]
        parts.append(jnp.where(kept, turned, 0.0))
    leg_all[my_af] = jnp.concatenate(parts, axis=0).astype(jnp.bfloat16)

    pl.semaphore_wait(barrier, devices - 1)

    for to_af in af_peers[1:]:
        pltpu.make_async_remote_copy(
            src_ref=leg_all.at[my_af],
            dst_ref=leg_all.at[my_af],
            send_sem=send_sems.at[0],
            recv_sem=recv_sems.at[0],
            device_id=(my_wa, to_af),
            device_id_type=MESH,
        ).start()

    placed[...] = jnp.zeros_like(placed)
    for load in loads[1:]:
        load.wait()
    for s in range(slots):
        placed[s, pl.ds(pl.multiple_of(my_af * cols, cols), cols), :] = spectra_ref[s]
    four_rows[...] = jnp.zeros_like(four_rows)

    points_int = points_smem[0]
    points = points_int.astype(jnp.float32)
    points_vec = jnp.full((1, 1), points, jnp.float32)
    first_lon = my_af * lon_count
    waves_row = wave_ref[...].astype(jnp.float32)

    def fill_tables(chunk, carry):
        row = iota((CHUNK, waves_total), 0)
        slot = lax.rem(row, SLOT_PAD)
        named = iota((CHUNK, waves_total), 1) == (
            (lax.div(row, SLOT_PAD) + chunk * CHUNK_WA) * slots + slot
        )
        named = jnp.logical_and(named, slot < slots)
        waves = jnp.sum(jnp.where(named, waves_row, 0.0), axis=1, keepdims=True)
        lane = iota((1, LANES), 1)
        base_cos, base_sin = cos_sin(waves, lane.astype(jnp.float32), points_vec)
        starts = (first_lon + LANES * lane).astype(jnp.float32)
        start_cos, start_sin = cos_sin(waves, starts, points_vec)
        for block in range(lon_count // LANES):
            part = pl.ds(block * LANES, LANES)
            c0 = start_cos[:, block : block + 1]
            s0 = start_sin[:, block : block + 1]
            tables[chunk, pl.ds(0, CHUNK), part] = (base_cos * c0 - base_sin * s0).astype(
                jnp.bfloat16
            )
            tables[chunk, pl.ds(CHUNK, CHUNK), part] = (
                -(base_sin * c0) - base_cos * s0
            ).astype(jnp.bfloat16)
        return carry

    if chunks == 1:
        fill_tables(0, 0)
    else:
        lax.fori_loop(0, chunks, fill_tables, 0)

    leg_bytes = leg_all.at[pl.ds(0, af_count - 1)]
    pltpu.make_async_copy(leg_bytes, leg_bytes, recv_sems.at[0]).wait()

    for s in range(slots):
        rows = pl.ds(s * lat_count, lat_count)
        full = leg_all[0, rows, :].astype(jnp.float32)
        for other in range(1, af_count):
            full = full + leg_all[other, rows, :].astype(jnp.float32)
        four_rows[pl.ds(s, lat_count, stride=SLOT_PAD), :] = dot(
            full.astype(jnp.bfloat16), placed[s], 1, 1
        )
    four_send[...] = four_rows[...].astype(jnp.bfloat16).reshape(four_send.shape)

    def send_fourier(to_wa, to_af):
        pltpu.make_async_remote_copy(
            src_ref=four_send.at[to_wa],
            dst_ref=four_recv.at[my_block],
            send_sem=send_sems.at[1],
            recv_sem=recv_sems.at[1],
            device_id=(to_wa, to_af),
            device_id_type=MESH,
        ).start()

    each_partner(send_fourier)
    four_recv[my_block] = four_send[my_wa]

    longitudes = first_lon + iota((1, lon_count), 1)
    in_row = (longitudes < points_int).astype(jnp.float32)
    usable = in_row * land_ref[...].astype(jnp.float32)
    soil_kinds = params_ref.shape[1]
    plant_kinds = roots_ref.shape[1]
    soil_hot = (iota((soil_kinds, lon_count), 0) == soil_ref[...]).astype(jnp.float32)
    plant_hot = (iota((plant_kinds, lon_count), 0) == plant_ref[...]).astype(jnp.float32)
    soil = dot(params_ref[...], soil_hot, 1, 0, HIGHEST)
    wilting = 0.04 + 0.1 * soil[0:1]
    capacity = 0.3 + 0.15 * soil[1:2]
    roots = roots_ref[...]
    fractions = roots / jnp.sum(roots, axis=0, keepdims=True)
    root_share = dot(fractions, plant_hot, 1, 0, HIGHEST)
    moisture = water_ref[0]
    excess = moisture - wilting
    factor = jnp.clip(excess / (capacity - wilting), 0.0, 1.0)
    share_factor = root_share * factor
    stress = jnp.sum(share_factor, axis=0, keepdims=True)
    layer = iota((SOIL_LAYERS, 1), 0)
    depths = jnp.full((SOIL_LAYERS, 1), DEPTHS[0], jnp.float32)
    for number in range(1, SOIL_LAYERS):
        depths = jnp.where(layer == number, DEPTHS[number], depths)
    reserve = jnp.sum(root_share * depths * jnp.maximum(excess, 0.0), axis=0, keepdims=True)
    available = usable * reserve

    four_bytes = four_recv.at[pl.ds(0, devices - 1)]
    pltpu.make_async_copy(four_bytes, four_bytes, recv_sems.at[1]).wait()

    def synthesize(chunk, total):
        summed = jnp.zeros((CHUNK, LANES), jnp.float32)
        for other in range(af_count):
            got = four_recv[pl.ds(other * wa_count + chunk * CHUNK_WA, CHUNK_WA)]
            summed = summed + got.reshape(CHUNK, LANES).astype(jnp.float32)
        turned = summed.T
        real = [turned[cols * g : cols * g + group] for g in range(af_count)]
        imag = [turned[cols * g + group : cols * (g + 1)] for g in range(af_count)]
        both = jnp.concatenate(
            [jnp.concatenate(real, axis=0), jnp.concatenate(imag, axis=0)], axis=1
        ).astype(jnp.bfloat16)
        return total + dot(both, tables[chunk], 1, 0)

    fields = jnp.zeros((group * af_count, lon_count), jnp.float32)
    if chunks == 1:
        fields = synthesize(0, fields)
    else:
        fields = lax.fori_loop(0, chunks, synthesize, fields)
    rounded = (fields * in_row * (1.0 / math.sqrt(waves_total))).astype(jnp.bfloat16)
    grid_ref[0] = rounded
    grid_write = pltpu.make_async_copy(grid_ref, grid_hbm, load_sems.at[len(loads)])
    grid_write.start()
    values = rounded.astype(jnp.float32)

    def lowest(field):
        return values[(field + 1) * LEVELS - 1 : (field + 1) * LEVELS]

    wind_u, wind_v, air, humid, skin = [lowest(f) for f in range(5)]
    speed = jnp.sqrt(1.0 + wind_u * wind_u + wind_v * wind_v)
    gap = air - humid
    softplus = jnp.maximum(gap, 0.0) + jnp.log1p(jnp.exp(-jnp.abs(gap)))
    demand = usable * (0.5 * speed * softplus)
    transpiration = demand * stress
    moving = in_row * speed
    fluxes = (transpiration, moving * (skin - air), moving * wind_u, moving * wind_v)
    nothing = jnp.zeros_like(demand)
    even, odd = [], []
    for flux in fluxes:
        even += [flux, nothing]
        odd += [nothing, flux]
    even = jnp.concatenate(even, axis=0)
    odd = jnp.concatenate(odd, axis=0)
    even = jnp.concatenate([even] * SLOT_PAD, axis=0).astype(jnp.bfloat16)
    odd = jnp.concatenate([odd] * SLOT_PAD, axis=0).astype(jnp.bfloat16)
    weight = weight_smem[0]
    area = weight / points_vec
    transpired = jnp.sum(transpiration, axis=1, keepdims=True) * area
    reserved = jnp.sum(available, axis=1, keepdims=True) * area
    row_scale = weight * lax.rsqrt(points_vec)

    rows8 = 2 * FLUXES
    first_spare = slots * rows8

    def analyse(chunk, carry):
        product = dot(tables[chunk, pl.ds(0, CHUNK), :], even, 1, 1) + dot(
            tables[chunk, pl.ds(CHUNK, CHUNK), :], odd, 1, 1
        )
        slot = lax.rem(iota((CHUNK, LANES), 0), SLOT_PAD)
        lane = iota((CHUNK, LANES), 1)
        mine = jnp.logical_and(lax.div(lane, rows8) == slot, slot < slots)
        kept = jnp.where(mine, product, 0.0).reshape(CHUNK_WA, SLOT_PAD, LANES)
        line = jnp.sum(kept, axis=1) * row_scale
        lane = iota((CHUNK_WA, LANES), 1)
        line = jnp.where(lane == first_spare, transpired, line)
        line = jnp.where(lane == first_spare + 1, reserved, line)
        coef_send[pl.ds(chunk * CHUNK_WA, CHUNK_WA)] = line.reshape(CHUNK_WA, 1, LANES)
        return carry

    if chunks == 1:
        analyse(0, 0)
    else:
        lax.fori_loop(0, chunks, analyse, 0)

    def send_coeffs(to_wa, to_af):
        pltpu.make_async_remote_copy(
            src_ref=coef_send.at[to_wa],
            dst_ref=coef_recv.at[my_block],
            send_sem=send_sems.at[2],
            recv_sem=recv_sems.at[2],
            device_id=(to_wa, to_af),
            device_id_type=MESH,
        ).start()

    each_partner(send_coeffs)
    coef_recv[my_block] = coef_send[my_wa]
    unfixed = demand * share_factor
    pltpu.make_async_copy(leg_bytes, leg_bytes, send_sems.at[0]).wait()
    pltpu.make_async_copy(four_bytes, four_bytes, send_sems.at[1]).wait()

    coef_bytes = coef_recv.at[pl.ds(0, devices - 1)]
    pltpu.make_async_copy(coef_bytes, coef_bytes, recv_sems.at[2]).wait()

    lines = coef_recv[pl.ds(0, wa_count)]
    for other in range(1, af_count):
        lines = lines + coef_recv[pl.ds(other * wa_count, wa_count)]
    lines = lines.reshape(wa_count, LANES)
    totals = jnp.sum(lines, axis=0, keepdims=True)
    fix_ratio = UPTAKE_SHARE * totals[:, first_spare + 1 : first_spare + 2] / (
        totals[:, first_spare : first_spare + 1]
    )
    uptake_ref[0] = fix_ratio * unfixed
    scaled = jnp.where(lax.rem(iota((1, LANES), 1), rows8) < 2, fix_ratio, 1.0) * lines
    turned = scaled.T
    offset = iota((rows8, n_local), 1) + my_af * n_local
    for s in range(slots):
        weighted = turned[s * rows8 : (s + 1) * rows8].astype(jnp.bfloat16)
        result = dot(weighted, legendre_ref[s], 1, 0)
        kept = offset < waves_total - wave_smem[my_wa * slots + s]
        spectral_ref[s] = jnp.where(kept, result, 0.0)

    pltpu.make_async_copy(coef_bytes, coef_bytes, send_sems.at[2]).wait()
    grid_write.wait()


def per_device(
    spectra,
    legendre,
    wave_of_slot,
    row_points,
    row_weight,
    soil_water,
    land_mask,
    soil_type,
    plant_type,
    soil_params,
    root_profile,
):
    wa_count = lax.axis_size("wa")
    af_count = lax.axis_size("af")
    slots, offsets, cols = spectra.shape
    n_local, lat_count = legendre.shape[1:]
    waves_total = wave_of_slot.shape[0]
    lon_count = soil_water.shape[2]
    devices = wa_count * af_count
    chunks = wa_count // CHUNK_WA
    assert row_points.shape[0] == 1 and lat_count == wa_count and cols * af_count == LANES
    assert slots * 2 * FLUXES + 2 <= LANES and slots <= SLOT_PAD
    assert wa_count % CHUNK_WA == 0 and lon_count % LANES == 0
    vmem = pl.BlockSpec(memory_space=pltpu.VMEM)
    smem = pl.BlockSpec(memory_space=pltpu.SMEM)
    operands = (
        legendre.transpose(0, 2, 1),
        spectra.transpose(0, 2, 1),
        wave_of_slot.reshape(1, waves_total),
        soil_water,
        land_mask,
        soil_type,
        plant_type,
        soil_params,
        root_profile.T,
    )
    hbm = pl.BlockSpec(memory_space=pltpu.HBM)
    results = pl.pallas_call(
        functools.partial(kernel, wa_count, af_count),
        out_shape=(
            jax.ShapeDtypeStruct((1, cols // 2 * af_count, lon_count), jnp.bfloat16),
            jax.ShapeDtypeStruct((1, SOIL_LAYERS, lon_count), jnp.float32),
            jax.ShapeDtypeStruct((slots, 2 * FLUXES, n_local), jnp.float32),
        ),
        in_specs=[smem] * 3 + [hbm] * len(operands),
        out_specs=(hbm, vmem, vmem),
        scratch_shapes=[
            pltpu.VMEM((af_count, slots * lat_count, offsets), jnp.bfloat16),
            pltpu.VMEM((slots, LANES, offsets), jnp.bfloat16),
            pltpu.VMEM((lat_count * SLOT_PAD, LANES), jnp.float32),
            pltpu.VMEM((lat_count, SLOT_PAD, LANES), jnp.bfloat16),
            pltpu.VMEM((devices, SLOT_PAD, LANES), jnp.bfloat16),
            pltpu.VMEM((chunks, 2 * CHUNK, lon_count), jnp.bfloat16),
            pltpu.VMEM((wa_count, 1, LANES), jnp.float32),
            pltpu.VMEM((devices, 1, LANES), jnp.float32),
            *[pltpu.VMEM(operand.shape, operand.dtype) for operand in operands],
            pltpu.VMEM((1, cols // 2 * af_count, lon_count), jnp.bfloat16),
            pltpu.SemaphoreType.DMA((3,)),
            pltpu.SemaphoreType.DMA((3,)),
            pltpu.SemaphoreType.DMA((len(operands) + 1,)),
        ],
        compiler_params=pltpu.CompilerParams(
            collective_id=0,
            has_side_effects=True,
            vmem_limit_bytes=VMEM_LIMIT,
        ),
    )(wave_of_slot, row_points, row_weight, *operands)
    return pl.pallas_call(
        write_out,
        out_shape=tuple(jax.ShapeDtypeStruct(r.shape, r.dtype) for r in results),
        in_specs=[pl.BlockSpec(memory_space=pl.ANY)] * len(results),
        out_specs=(hbm,) * len(results),
        scratch_shapes=[pltpu.SemaphoreType.DMA((len(results),))],
        compiler_params=pltpu.CompilerParams(vmem_limit_bytes=VMEM_LIMIT),
    )(*results)


def write_out(grid_in, uptake_in, spectral_in, grid_out, uptake_out, spectral_out, sems):
    copies = [
        pltpu.make_async_copy(source, target, sems.at[number])
        for number, (source, target) in enumerate(
            ((grid_in, grid_out), (uptake_in, uptake_out), (spectral_in, spectral_out))
        )
    ]
    for copy in copies:
        copy.start()
    for copy in copies:
        copy.wait()


def solution(mesh):
    in_specs = (
        P("wa", None, "af"),
        P("wa", "af", None),
        P(),
        P("wa"),
        P("wa"),
        P("wa", None, "af"),
        P("wa", "af"),
        P("wa", "af"),
        P("wa", "af"),
        P(),
        P(),
    )
    out_specs = (P("wa", None, "af"), P("wa", None, "af"), P("wa", None, "af"))
    return jax.shard_map(
        per_device, mesh=mesh, in_specs=in_specs, out_specs=out_specs, check_vma=False
    )
```

```python
import functools
import math

import jax
import jax.numpy as jnp
from jax import lax
from jax.experimental import pallas as pl
from jax.experimental.pallas import tpu as pltpu
from jax.sharding import PartitionSpec as P

LEVELS = 8
FLUXES = 4
SOIL_LAYERS = 4
TWO_PI = 2.0 * math.pi
DEPTHS = (0.07, 0.21, 0.72, 1.89)
UPTAKE_SHARE = 4.0
MESH = pl.DeviceIdType.MESH
HIGHEST = lax.Precision.HIGHEST
SLOT_PAD = 16
CHUNK_WA = 8
CHUNK = SLOT_PAD * CHUNK_WA
LANES = 128
VMEM_LIMIT = 56 * 1024 * 1024


def dot(lhs, rhs, lhs_dim, rhs_dim, precision=None):
    return lax.dot_general(
        lhs,
        rhs,
        (((lhs_dim,), (rhs_dim,)), ((), ())),
        precision=precision,
        preferred_element_type=jnp.float32,
    )


def iota(shape, dim):
    return lax.broadcasted_iota(jnp.int32, shape, dim)


def cos_sin(waves, longitudes, points):
    product = waves * longitudes
    residue = product - points * jnp.round(product * (1.0 / points))
    quarters = residue * (4.0 / points)
    quadrant = jnp.round(quarters)
    angle = (quarters - quadrant) * (0.25 * TWO_PI)
    square = angle * angle
    cosine = 1.0 + square * (
        -1 / 2 + square * (1 / 24 + square * (-1 / 720 + square * (1 / 40320)))
    )
    sine = angle * (
        1.0 + square * (-1 / 6 + square * (1 / 120 + square * (-1 / 5040 + square * (1 / 362880))))
    )
    size = jnp.abs(quadrant)
    odd = size == 1.0
    sign = 1.0 - size
    return (
        jnp.where(odd, -quadrant * sine, sign * cosine),
        jnp.where(odd, quadrant * cosine, sign * sine),
    )


def kernel(
    wa_count,
    af_count,
    wave_smem,
    points_smem,
    weight_smem,
    legendre_hbm,
    spectra_hbm,
    wave_hbm,
    water_hbm,
    land_hbm,
    soil_hbm,
    plant_hbm,
    params_hbm,
    roots_hbm,
    grid_hbm,
    uptake_ref,
    spectral_ref,
    leg_all,
    placed,
    four_rows,
    four_send,
    four_recv,
    tables,
    coef_send,
    coef_recv,
    legendre_ref,
    spectra_ref,
    wave_ref,
    water_ref,
    land_ref,
    soil_ref,
    plant_ref,
    params_ref,
    roots_ref,
    grid_ref,
    send_sems,
    recv_sems,
    load_sems,
):
    slots, cols, offsets = spectra_ref.shape
    lat_count = legendre_ref.shape[1]
    n_local = legendre_ref.shape[2]
    waves_total = wave_ref.shape[1]
    lon_count = water_ref.shape[2]
    group = cols // 2
    devices = wa_count * af_count
    chunks = wa_count // CHUNK_WA
    my_wa = lax.axis_index("wa")
    my_af = lax.axis_index("af")
    my_block = my_af * wa_count + my_wa

    def wrapped(index, count):
        return jnp.where(index >= count, index - count, index)

    af_peers = [my_af] + [wrapped(my_af + step, af_count) for step in range(1, af_count)]

    def each_partner(act):
        def row(step, carry):
            to_wa = wrapped(my_wa + step, wa_count)
            for to_af in af_peers:
                act(to_wa, to_af)
            return carry

        lax.fori_loop(1, wa_count, row, 0)
        for to_af in af_peers[1:]:
            act(my_wa, to_af)

    barrier = pltpu.get_barrier_semaphore()

    def greet(to_wa, to_af):
        pl.semaphore_signal(barrier, inc=1, device_id=(to_wa, to_af), device_id_type=MESH)

    loads = [
        pltpu.make_async_copy(source, target, load_sems.at[number])
        for number, (source, target) in enumerate(
            (
                (legendre_hbm, legendre_ref),
                (spectra_hbm, spectra_ref),
                (wave_hbm, wave_ref),
                (water_hbm, water_ref),
                (land_hbm, land_ref),
                (soil_hbm, soil_ref),
                (plant_hbm, plant_ref),
                (params_hbm, params_ref),
                (roots_hbm, roots_ref),
            )
        )
    ]
    loads[0].start()
    each_partner(greet)
    for load in loads[1:]:
        load.start()
    loads[0].wait()

    place = (
        iota((n_local, offsets), 1) == iota((n_local, offsets), 0) + my_af * n_local
    ).astype(jnp.float32).astype(jnp.bfloat16)
    lane_offset = iota((lat_count, offsets), 1)
    parts = []
    for s in range(slots):
        turned = dot(legendre_ref[s], place, 1, 0)
        kept = lane_offset < waves_total - wave_smem[my_wa * slots + s]
        parts.append(jnp.where(kept, turned, 0.0))
    leg_all[my_af] = jnp.concatenate(parts, axis=0).astype(jnp.bfloat16)

    pl.semaphore_wait(barrier, devices - 1)

    for to_af in af_peers[1:]:
        pltpu.make_async_remote_copy(
            src_ref=leg_all.at[my_af],
            dst_ref=leg_all.at[my_af],
            send_sem=send_sems.at[0],
            recv_sem=recv_sems.at[0],
            device_id=(my_wa, to_af),
            device_id_type=MESH,
        ).start()

    placed[...] = jnp.zeros_like(placed)
    for load in loads[1:]:
        load.wait()
    for s in range(slots):
        placed[s, pl.ds(pl.multiple_of(my_af * cols, cols), cols), :] = spectra_ref[s]
    four_rows[...] = jnp.zeros_like(four_rows)

    points_int = points_smem[0]
    points = points_int.astype(jnp.float32)
    points_vec = jnp.full((1, 1), points, jnp.float32)
    first_lon = my_af * lon_count
    waves_row = wave_ref[...].astype(jnp.float32)

    def fill_tables(chunk, carry):
        row = iota((CHUNK, waves_total), 0)
        slot = lax.rem(row, SLOT_PAD)
        named = iota((CHUNK, waves_total), 1) == (
            (lax.div(row, SLOT_PAD) + chunk * CHUNK_WA) * slots + slot
        )
        named = jnp.logical_and(named, slot < slots)
        waves = jnp.sum(jnp.where(named, waves_row, 0.0), axis=1, keepdims=True)
        lane = iota((1, LANES), 1)
        base_cos, base_sin = cos_sin(waves, lane.astype(jnp.float32), points_vec)
        starts = (first_lon + LANES * lane).astype(jnp.float32)
        start_cos, start_sin = cos_sin(waves, starts, points_vec)
        for block in range(lon_count // LANES):
            part = pl.ds(block * LANES, LANES)
            c0 = start_cos[:, block : block + 1]
            s0 = start_sin[:, block : block + 1]
            tables[chunk, pl.ds(0, CHUNK), part] = (base_cos * c0 - base_sin * s0).astype(
                jnp.bfloat16
            )
            tables[chunk, pl.ds(CHUNK, CHUNK), part] = (
                -(base_sin * c0) - base_cos * s0
            ).astype(jnp.bfloat16)
        return carry

    if chunks == 1:
        fill_tables(0, 0)
    else:
        lax.fori_loop(0, chunks, fill_tables, 0)

    leg_bytes = leg_all.at[pl.ds(0, af_count - 1)]
    pltpu.make_async_copy(leg_bytes, leg_bytes, recv_sems.at[0]).wait()

    for s in range(slots):
        rows = pl.ds(s * lat_count, lat_count)
        full = leg_all[0, rows, :].astype(jnp.float32)
        for other in range(1, af_count):
            full = full + leg_all[other, rows, :].astype(jnp.float32)
        four_rows[pl.ds(s, lat_count, stride=SLOT_PAD), :] = dot(
            full.astype(jnp.bfloat16), placed[s], 1, 1
        )
    four_send[...] = four_rows[...].astype(jnp.bfloat16).reshape(four_send.shape)

    def send_fourier(to_wa, to_af):
        pltpu.make_async_remote_copy(
            src_ref=four_send.at[to_wa],
            dst_ref=four_recv.at[my_block],
            send_sem=send_sems.at[1],
            recv_sem=recv_sems.at[1],
            device_id=(to_wa, to_af),
            device_id_type=MESH,
        ).start()

    each_partner(send_fourier)
    four_recv[my_block] = four_send[my_wa]

    longitudes = first_lon + iota((1, lon_count), 1)
    in_row = (longitudes < points_int).astype(jnp.float32)
    usable = in_row * land_ref[...].astype(jnp.float32)
    soil_kinds = params_ref.shape[1]
    plant_kinds = roots_ref.shape[1]
    soil_hot = (iota((soil_kinds, lon_count), 0) == soil_ref[...]).astype(jnp.float32)
    plant_hot = (iota((plant_kinds, lon_count), 0) == plant_ref[...]).astype(jnp.float32)
    soil = dot(params_ref[...], soil_hot, 1, 0, HIGHEST)
    wilting = 0.04 + 0.1 * soil[0:1]
    capacity = 0.3 + 0.15 * soil[1:2]
    roots = roots_ref[...]
    fractions = roots / jnp.sum(roots, axis=0, keepdims=True)
    root_share = dot(fractions, plant_hot, 1, 0, HIGHEST)
    moisture = water_ref[0]
    excess = moisture - wilting
    factor = jnp.clip(excess / (capacity - wilting), 0.0, 1.0)
    share_factor = root_share * factor
    stress = jnp.sum(share_factor, axis=0, keepdims=True)
    layer = iota((SOIL_LAYERS, 1), 0)
    depths = jnp.full((SOIL_LAYERS, 1), DEPTHS[0], jnp.float32)
    for number in range(1, SOIL_LAYERS):
        depths = jnp.where(layer == number, DEPTHS[number], depths)
    reserve = jnp.sum(root_share * depths * jnp.maximum(excess, 0.0), axis=0, keepdims=True)
    available = usable * reserve

    four_bytes = four_recv.at[pl.ds(0, devices - 1)]
    pltpu.make_async_copy(four_bytes, four_bytes, recv_sems.at[1]).wait()

    def synthesize(chunk, total):
        summed = jnp.zeros((CHUNK, LANES), jnp.float32)
        for other in range(af_count):
            got = four_recv[pl.ds(other * wa_count + chunk * CHUNK_WA, CHUNK_WA)]
            summed = summed + got.reshape(CHUNK, LANES).astype(jnp.float32)
        turned = summed.T
        real = [turned[cols * g : cols * g + group] for g in range(af_count)]
        imag = [turned[cols * g + group : cols * (g + 1)] for g in range(af_count)]
        both = jnp.concatenate(
            [jnp.concatenate(real, axis=0), jnp.concatenate(imag, axis=0)], axis=1
        ).astype(jnp.bfloat16)
        return total + dot(both, tables[chunk], 1, 0)

    fields = jnp.zeros((group * af_count, lon_count), jnp.float32)
    if chunks == 1:
        fields = synthesize(0, fields)
    else:
        fields = lax.fori_loop(0, chunks, synthesize, fields)
    rounded = (fields * in_row * (1.0 / math.sqrt(waves_total))).astype(jnp.bfloat16)
    grid_ref[0] = rounded
    grid_write = pltpu.make_async_copy(grid_ref, grid_hbm, load_sems.at[len(loads)])
    grid_write.start()
    values = rounded.astype(jnp.float32)

    def lowest(field):
        return values[(field + 1) * LEVELS - 1 : (field + 1) * LEVELS]

    wind_u, wind_v, air, humid, skin = [lowest(f) for f in range(5)]
    speed = jnp.sqrt(1.0 + wind_u * wind_u + wind_v * wind_v)
    gap = air - humid
    softplus = jnp.maximum(gap, 0.0) + jnp.log1p(jnp.exp(-jnp.abs(gap)))
    demand = usable * (0.5 * speed * softplus)
    transpiration = demand * stress
    moving = in_row * speed
    fluxes = (transpiration, moving * (skin - air), moving * wind_u, moving * wind_v)
    nothing = jnp.zeros_like(demand)
    even, odd = [], []
    for flux in fluxes:
        even += [flux, nothing]
        odd += [nothing, flux]
    even = jnp.concatenate(even, axis=0)
    odd = jnp.concatenate(odd, axis=0)
    even = jnp.concatenate([even] * SLOT_PAD, axis=0).astype(jnp.bfloat16)
    odd = jnp.concatenate([odd] * SLOT_PAD, axis=0).astype(jnp.bfloat16)
    weight = weight_smem[0]
    area = weight / points_vec
    transpired = jnp.sum(transpiration, axis=1, keepdims=True) * area
    reserved = jnp.sum(available, axis=1, keepdims=True) * area
    row_scale = weight * lax.rsqrt(points_vec)

    rows8 = 2 * FLUXES
    first_spare = slots * rows8

    def analyse(chunk, carry):
        product = dot(tables[chunk, pl.ds(0, CHUNK), :], even, 1, 1) + dot(
            tables[chunk, pl.ds(CHUNK, CHUNK), :], odd, 1, 1
        )
        slot = lax.rem(iota((CHUNK, LANES), 0), SLOT_PAD)
        lane = iota((CHUNK, LANES), 1)
        mine = jnp.logical_and(lax.div(lane, rows8) == slot, slot < slots)
        kept = jnp.where(mine, product, 0.0).reshape(CHUNK_WA, SLOT_PAD, LANES)
        line = jnp.sum(kept, axis=1) * row_scale
        lane = iota((CHUNK_WA, LANES), 1)
        line = jnp.where(lane == first_spare, transpired, line)
        line = jnp.where(lane == first_spare + 1, reserved, line)
        coef_send[pl.ds(chunk * CHUNK_WA, CHUNK_WA)] = line.reshape(CHUNK_WA, 1, LANES)
        return carry

    if chunks == 1:
        analyse(0, 0)
    else:
        lax.fori_loop(0, chunks, analyse, 0)

    def send_coeffs(to_wa, to_af):
        pltpu.make_async_remote_copy(
            src_ref=coef_send.at[to_wa],
            dst_ref=coef_recv.at[my_block],
            send_sem=send_sems.at[2],
            recv_sem=recv_sems.at[2],
            device_id=(to_wa, to_af),
            device_id_type=MESH,
        ).start()

    each_partner(send_coeffs)
    coef_recv[my_block] = coef_send[my_wa]
    unfixed = demand * share_factor
    pltpu.make_async_copy(leg_bytes, leg_bytes, send_sems.at[0]).wait()
    pltpu.make_async_copy(four_bytes, four_bytes, send_sems.at[1]).wait()

    coef_bytes = coef_recv.at[pl.ds(0, devices - 1)]
    pltpu.make_async_copy(coef_bytes, coef_bytes, recv_sems.at[2]).wait()

    lines = coef_recv[pl.ds(0, wa_count)]
    for other in range(1, af_count):
        lines = lines + coef_recv[pl.ds(other * wa_count, wa_count)]
    lines = lines.reshape(wa_count, LANES)
    totals = jnp.sum(lines, axis=0, keepdims=True)
    fix_ratio = UPTAKE_SHARE * totals[:, first_spare + 1 : first_spare + 2] / (
        totals[:, first_spare : first_spare + 1]
    )
    uptake_ref[0] = fix_ratio * unfixed
    scaled = jnp.where(lax.rem(iota((1, LANES), 1), rows8) < 2, fix_ratio, 1.0) * lines
    turned = scaled.T
    offset = iota((rows8, n_local), 1) + my_af * n_local
    for s in range(slots):
        weighted = turned[s * rows8 : (s + 1) * rows8].astype(jnp.bfloat16)
        result = dot(weighted, legendre_ref[s], 1, 0)
        kept = offset < waves_total - wave_smem[my_wa * slots + s]
        spectral_ref[s] = jnp.where(kept, result, 0.0)

    pltpu.make_async_copy(coef_bytes, coef_bytes, send_sems.at[2]).wait()
    grid_write.wait()


def per_device(
    spectra,
    legendre,
    wave_of_slot,
    row_points,
    row_weight,
    soil_water,
    land_mask,
    soil_type,
    plant_type,
    soil_params,
    root_profile,
):
    wa_count = lax.axis_size("wa")
    af_count = lax.axis_size("af")
    slots, offsets, cols = spectra.shape
    n_local, lat_count = legendre.shape[1:]
    waves_total = wave_of_slot.shape[0]
    lon_count = soil_water.shape[2]
    devices = wa_count * af_count
    chunks = wa_count // CHUNK_WA
    assert row_points.shape[0] == 1 and lat_count == wa_count and cols * af_count == LANES
    assert slots * 2 * FLUXES + 2 <= LANES and slots <= SLOT_PAD
    assert wa_count % CHUNK_WA == 0 and lon_count % LANES == 0
    vmem = pl.BlockSpec(memory_space=pltpu.VMEM)
    smem = pl.BlockSpec(memory_space=pltpu.SMEM)
    operands = (
        legendre.transpose(0, 2, 1),
        spectra.transpose(0, 2, 1),
        wave_of_slot.reshape(1, waves_total),
        soil_water,
        land_mask,
        soil_type,
        plant_type,
        soil_params,
        root_profile.T,
    )
    hbm = pl.BlockSpec(memory_space=pltpu.HBM)
    return pl.pallas_call(
        functools.partial(kernel, wa_count, af_count),
        out_shape=(
            jax.ShapeDtypeStruct((1, cols // 2 * af_count, lon_count), jnp.bfloat16),
            jax.ShapeDtypeStruct((1, SOIL_LAYERS, lon_count), jnp.float32),
            jax.ShapeDtypeStruct((slots, 2 * FLUXES, n_local), jnp.float32),
        ),
        in_specs=[smem] * 3 + [hbm] * len(operands),
        out_specs=(hbm, vmem, vmem),
        scratch_shapes=[
            pltpu.VMEM((af_count, slots * lat_count, offsets), jnp.bfloat16),
            pltpu.VMEM((slots, LANES, offsets), jnp.bfloat16),
            pltpu.VMEM((lat_count * SLOT_PAD, LANES), jnp.float32),
            pltpu.VMEM((lat_count, SLOT_PAD, LANES), jnp.bfloat16),
            pltpu.VMEM((devices, SLOT_PAD, LANES), jnp.bfloat16),
            pltpu.VMEM((chunks, 2 * CHUNK, lon_count), jnp.bfloat16),
            pltpu.VMEM((wa_count, 1, LANES), jnp.float32),
            pltpu.VMEM((devices, 1, LANES), jnp.float32),
            *[pltpu.VMEM(operand.shape, operand.dtype) for operand in operands],
            pltpu.VMEM((1, cols // 2 * af_count, lon_count), jnp.bfloat16),
            pltpu.SemaphoreType.DMA((3,)),
            pltpu.SemaphoreType.DMA((3,)),
            pltpu.SemaphoreType.DMA((len(operands) + 1,)),
        ],
        compiler_params=pltpu.CompilerParams(
            collective_id=0,
            has_side_effects=True,
            vmem_limit_bytes=VMEM_LIMIT,
        ),
    )(wave_of_slot, row_points, row_weight, *operands)

def solution(mesh):
    in_specs = (
        P("wa", None, "af"),
        P("wa", "af", None),
        P(),
        P("wa"),
        P("wa"),
        P("wa", None, "af"),
        P("wa", "af"),
        P("wa", "af"),
        P("wa", "af"),
        P(),
        P(),
    )
    out_specs = (P("wa", None, "af"), P("wa", None, "af"), P("wa", None, "af"))
    return jax.shard_map(
        per_device, mesh=mesh, in_specs=in_specs, out_specs=out_specs, check_vma=False
    )
```
